32 devices in a mesh: mode: 4 (over y, core), mesh: 8 (over z, x).
Axes of the slice: x: 2, y: 2, z: 4, core: 2. Of those that a mesh axis runs over, the one named last changes fastest.
Arguments:
- src_rows: bfloat16 [8192, 640], P(('mode', 'mesh')), parts along dimension 0, may hold values from -4 to 4
- src_owner: int32 [8192, 1], P(('mode', 'mesh')), parts along dimension 0, may hold values from 0 to 7; in each aligned block of 256 rows (0 to 255, 256 to 511, ...) at most 64 rows name the same one
- src_slot: int32 [8192], P(('mode', 'mesh')), parts along dimension 0, may hold values from 0 to 63
- neighbour_offset: int32 [2048, 6], P(('mode', 'mesh')), parts along dimension 0, may hold values from -16 to 16
- liner_face: int32 [2048], P(('mode', 'mesh')), parts along dimension 0, may hold values from 0 to 127
- admittance: float32 [8, 128], P('mode', 'mesh'), parts along dimension 0, may hold values from 0.2 to 1.5
- observe_weight: float32 [2048], P(('mode', 'mesh')), parts along dimension 0, may hold values from 0.3 to 3
- coupling: bfloat16 [24, 320, 640], P('mode'), parts along dimension 0, may hold values from -0.046875 to 0.046875
- block_inv: bfloat16 [1280, 640], P('mode'), parts along dimension 0, may hold values from -1.5 to 1.5, as said below
- liner_op: bfloat16 [1280, 640], P('mode'), parts along dimension 0, may hold values from -0.0625 to 0.0625
Outputs:
- state_field: bfloat16 [2048, 640], P(('mode', 'mesh')), parts along dimension 0
- adjoint_field: bfloat16 [2048, 640], P(('mode', 'mesh')), parts along dimension 0
- liner_grad: float32 [8, 128], P('mode', 'mesh'), parts along dimension 0
The draws below stay inside these ranges and needn't reach their ends.
There are 4 independent parts, one for each index of `mode`. The reference program is written for one: setup_inputs(seed, part) draws one part's arguments, and reference() takes and returns one part's arrays. A program takes and returns all parts, laid end to end along the dimension named above; each array names one. Nothing has to cross between parts.
Inputs may be any that keep to these rules, and one draw needn't show every extreme that they name: `src_owner`: in the rows of one device no owner is named by more than 64 rows, a bound that some block reaches. `block_inv`: real parts of the diagonal entries lie near 0.8; the rest is of order 320 ** -0.5.
All inputs are finite; a program needn't handle non-finite values.
Results may differ from the reference program's by a relative error of at most 0.018.
Values may be sent and summed in bfloat16 or wider, within the bound.
A program may use at most 64 MiB of HBM per device.

```python
import math
import jax
import jax.numpy as jnp
import numpy as np
from jax import lax

NB = 320
EL_DEV = 64
RIM = 16
SRC_DEV = 256
SWEEPS = 4
CAP = 64
ELEMS = 512
SOURCES = 2048
LFACES = 128
N_MESH = 8


def draw_block_inv(key, part):
    key_noise = jax.random.fold_in(key, 17)
    jitter = jnp.clip(jax.random.normal(key_noise, (NB, 2 * NB), jnp.float32), -4.0, 4.0)
    identity = jnp.concatenate([jnp.eye(NB, dtype=jnp.float32), jnp.zeros((NB, NB), jnp.float32)], axis=1)
    return (0.8 * identity + 0.6 / NB ** 0.5 * jitter).astype(jnp.bfloat16)


def touch_ends(entries, stream_key, low, largest):
    spot = [jax.random.randint(jax.random.fold_in(stream_key, axis), (), 0, length) for axis, length in enumerate(entries.shape)]
    longest = entries.shape.index(max(entries.shape))
    next_to = spot[:longest] + [(spot[longest] + 1) % entries.shape[longest]] + spot[longest + 1:]
    return entries.at[tuple(spot)].set(low).at[tuple(next_to)].set(largest)


def shard_levels(own_key, shape, cuts, least, top_value):
    level, own = 1.0, jax.random.fold_in(own_key, 6)
    for position, shards_of in cuts:
        heights = jnp.exp(jax.random.uniform(jax.random.fold_in(own, position), (shards_of,), jnp.float32, least / len(cuts), top_value / len(cuts)))
        level = level * jnp.repeat(heights, shape[position] // shards_of).reshape([-1 if axis == position else 1 for axis in range(len(shape))])
    return level


def routed_block(rng, own, number, rows, count, top, bound, lean):
    order = jax.random.permutation(rng, count)
    heavy_load, ordinary = load_shares(count, rows * top, bound, lean, True), load_shares(count, rows * top, bound, lean, False)
    places = jnp.arange(count)

    def named(tallies, offset_by):
        used = int((tallies > 0).sum())
        fixed = max(1, used // 4)
        moved = fixed + (places - fixed + offset_by * (used - fixed)) % max(1, count - fixed)
        return jnp.zeros((count,), jnp.int32).at[order[jnp.where(places < fixed, places, moved)]].set(jnp.asarray(tallies, jnp.int32))

    tallies = jnp.where(number % 4 == 0, named(heavy_load, number // 4), named(ordinary, number - number // 4 - 1))
    mixed = jax.random.permutation(jax.random.fold_in(own, 3), count)
    source_of, taker = mixed[0:count // 2 * 2:2], mixed[1:count // 2 * 2:2]
    margin = jnp.minimum(tallies[source_of] - 1, bound - tallies[taker]) // 2
    margin = jnp.where((source_of == order[0]) | (taker == order[0]) | (tallies[taker] == 0), 0, jnp.maximum(margin, 0))
    moved = jax.random.randint(jax.random.fold_in(own, 4), (count // 2,), 0, 1 << 20) % (margin + 1)
    tallies = tallies.at[source_of].add(-moved).at[taker].add(moved)
    members = jnp.searchsorted(jnp.cumsum(tallies), jnp.arange(rows * top), side="right").astype(jnp.int32)
    grid = members.reshape(top, rows).T
    grid = grid[jax.random.permutation(jax.random.fold_in(own, 1), rows)]
    offset_by = jax.random.randint(jax.random.fold_in(own, 2), (rows, 1), 0, top)
    return jnp.take_along_axis(grid, (jnp.arange(top)[None, :] + offset_by) % top, axis=1)


def load_shares(amount, total, bound, skew, full):
    weights = [(1 << 20) // math.isqrt(grade ** skew) + 1 for grade in range(1, amount + 1)]
    largest = bound if full else min(bound, max(-(-total // amount), total * weights[0] // sum(weights)))
    least = 1 if total - largest >= amount - 1 else 0
    counts, spare = [largest] + [least] * (amount - 1), total - largest - least * (amount - 1)
    while spare > 0:
        free = [i for i in range(1, amount) if counts[i] < largest] or [i for i in range(1, amount) if counts[i] < bound]
        pool, budget = sum([weights[i] for i in free]), spare
        for i in free:
            more = min(bound - counts[i], max(1, budget * weights[i] // pool), spare)
            counts[i] = counts[i] + more
            spare = spare - more
    return np.array(counts)


def scatter_about(rng, dims, scale, bound, split=(), held_as=jnp.bfloat16):
    gain = shard_levels(rng, dims, split, -0.22, 0.18) if split else 1.0
    result = jax.random.normal(rng, dims, jnp.float32) * scale * gain
    return jnp.minimum(jnp.maximum(result, -bound), bound).astype(held_as)


def setup_inputs(seed: int = 0, part: int = 0) -> dict:
    arg_keys = jax.random.split(jax.random.key(seed), 11)
    own_keys = jax.random.split(jax.random.fold_in(arg_keys[10], part), 11)
    src_rows = scatter_about(own_keys[0], (SOURCES, 2 * NB), 0.5, 4.0, ((0, 8),))
    src_owner_keys = jax.random.split(jax.random.fold_in(own_keys[1], 1), SOURCES // SRC_DEV)
    src_owner_turns = jax.random.permutation(jax.random.fold_in(own_keys[1], 3), SOURCES // SRC_DEV)
    src_owner = jax.vmap(lambda own, number: routed_block(jax.random.fold_in(own_keys[1], 2), own, number, SRC_DEV, N_MESH, 1, CAP, 2))(src_owner_keys, src_owner_turns).reshape((SOURCES, 1))
    src_slot = touch_ends(jax.random.randint(own_keys[2], (SOURCES,), 0, EL_DEV), jax.random.fold_in(own_keys[2], 1), 0, EL_DEV - 1).astype(jnp.int32)
    neighbour_offset = touch_ends(jax.random.randint(own_keys[3], (ELEMS, 6), -RIM, RIM + 1), jax.random.fold_in(own_keys[3], 1), -RIM, RIM).astype(jnp.int32)
    liner_face = touch_ends(jax.random.randint(own_keys[4], (ELEMS,), 0, LFACES), jax.random.fold_in(own_keys[4], 1), 0, LFACES - 1).astype(jnp.int32)
    admittance = jnp.clip(0.2 + 1.3 * jax.random.uniform(own_keys[5], (2, LFACES), jnp.float32) ** shard_levels(own_keys[5], (2, LFACES), ((1, 8),), -0.2, 0.2), 0.2, 1.5)
    observe_weight = jnp.clip(jnp.exp(math.log(3.0) - 2.3025851 * jax.random.uniform(own_keys[6], (ELEMS,), jnp.float32) ** shard_levels(own_keys[6], (ELEMS,), ((0, 8),), -0.2, 0.2)), 0.3, 3.0)
    coupling = scatter_about(own_keys[7], (6, NB, 2 * NB), (48 * NB) ** -0.5, 0.046875)
    block_inv = draw_block_inv(jax.random.fold_in(jax.random.fold_in(arg_keys[10], part), 71), part)
    liner_op = scatter_about(own_keys[9], (NB, 2 * NB), (32 * NB) ** -0.5, 0.0625)
    return {"src_rows": src_rows, "src_owner": src_owner, "src_slot": src_slot, "neighbour_offset": neighbour_offset, "liner_face": liner_face, "admittance": admittance, "observe_weight": observe_weight, "coupling": coupling, "block_inv": block_inv, "liner_op": liner_op}


def complex_apply(rows_in, matrix):
    half_width = matrix.shape[0]
    row_count = rows_in.shape[0]
    stacked = jnp.concatenate([rows_in[:, :half_width], rows_in[:, half_width:]], axis=0)
    product = jnp.dot(stacked, matrix, preferred_element_type=jnp.float32)
    upper_half = product[:row_count]
    lower_half = product[row_count:]
    return jnp.concatenate([upper_half[:, :half_width] - lower_half[:, half_width:], upper_half[:, half_width:] + lower_half[:, :half_width]], axis=1)


def hermitian_apply(rows_in, matrix):
    half_width = matrix.shape[0]
    row_count = rows_in.shape[0]
    swapped = jnp.concatenate([rows_in[:, half_width:], -rows_in[:, :half_width]], axis=1)
    stacked = jnp.concatenate([rows_in, swapped], axis=0)
    product = lax.dot_general(stacked, matrix, (((1,), (1,)), ((), ())), preferred_element_type=jnp.float32)
    return jnp.concatenate([product[:row_count], product[row_count:]], axis=1)


def wall_term(wall_wave, resist, reactance, conjugate):
    half_width = wall_wave.shape[1] // 2
    real_part = wall_wave[:, :half_width]
    imag_part = wall_wave[:, half_width:]
    sign_value = -1.0 if conjugate else 1.0
    resist = resist[:, None]
    reactance = sign_value * reactance[:, None]
    return jnp.concatenate([resist * real_part - reactance * imag_part, resist * imag_part + reactance * real_part], axis=1)


def reference(src_rows, src_owner, src_slot, neighbour_offset, liner_face, admittance, observe_weight, coupling, block_inv, liner_op):
    elem_total = EL_DEV * N_MESH
    target = (src_owner[:, 0] * EL_DEV + src_slot).astype(jnp.int32)
    forcing = jnp.zeros((elem_total, 2 * NB), jnp.float32).at[target].add(src_rows.astype(jnp.float32))
    resist = jnp.take(admittance[0], liner_face)
    reactance = jnp.take(admittance[1], liner_face)
    face_index = (jnp.arange(elem_total, dtype=jnp.int32)[:, None] + RIM + neighbour_offset).astype(jnp.int32)
    state_field = complex_apply(forcing.astype(jnp.bfloat16), block_inv).astype(jnp.bfloat16)
    for sweep_step in range(SWEEPS):
        padded = jnp.pad(state_field, ((RIM, RIM), (0, 0)))
        residual_sum = forcing - wall_term(complex_apply(state_field, liner_op), resist, reactance, False)
        for face_dir in range(6):
            residual_sum = residual_sum - complex_apply(jnp.take(padded, face_index[:, face_dir], axis=0), coupling[face_dir])
        state_field = complex_apply(residual_sum.astype(jnp.bfloat16), block_inv).astype(jnp.bfloat16)
    source = observe_weight[:, None] * state_field.astype(jnp.float32)
    adjoint_field = hermitian_apply(source.astype(jnp.bfloat16), block_inv).astype(jnp.bfloat16)
    for sweep_step in range(SWEEPS):
        spread = jnp.zeros((elem_total + 2 * RIM, 2 * NB), jnp.float32)
        for face_dir in range(6):
            spread = spread.at[face_index[:, face_dir]].add(hermitian_apply(adjoint_field, coupling[face_dir]))
        residual_sum = source - spread[RIM:RIM + elem_total] - wall_term(hermitian_apply(adjoint_field, liner_op), resist, reactance, True)
        adjoint_field = hermitian_apply(residual_sum.astype(jnp.bfloat16), block_inv).astype(jnp.bfloat16)
    wall_wave = complex_apply(state_field, liner_op)
    adjoint_f = adjoint_field.astype(jnp.float32)
    term_re = -jnp.sum(adjoint_f[:, :NB] * wall_wave[:, :NB] + adjoint_f[:, NB:] * wall_wave[:, NB:], axis=1) / 16.0
    term_im = -jnp.sum(adjoint_f[:, NB:] * wall_wave[:, :NB] - adjoint_f[:, :NB] * wall_wave[:, NB:], axis=1) / 16.0
    liner_grad = jnp.zeros((2, LFACES), jnp.float32)
    liner_grad = liner_grad.at[0, liner_face].add(term_re).at[1, liner_face].add(term_im)
    return state_field, adjoint_field, liner_grad
```

```python
import functools

import jax
import jax.numpy as jnp
from jax import lax
from jax.experimental import pallas as pl
from jax.experimental.pallas import tpu as pltpu
from jax.sharding import PartitionSpec as P

SWEEPS = 4
RIM = 16
FACES = 6
HALF = 384
FULL = 2 * HALF
MESH = pl.DeviceIdType.MESH
F32 = jnp.float32
BF16 = jnp.bfloat16


def iota(shape, dim):
    return lax.broadcasted_iota(jnp.int32, shape, dim)


def dot(a, b):
    return jnp.dot(a, b, preferred_element_type=F32)


def widen(x, nb):
    rows = x.shape[0]
    turned = pltpu.roll(x, HALF - nb, 1)
    wrap = 2 * (HALF - nb)
    real = jnp.where(iota((rows, HALF), 1) < nb, x[:, :HALF], 0.0)
    last = jnp.where(iota((rows, wrap), 1) < HALF - nb, turned[:, :wrap], 0.0)
    return jnp.concatenate([real, turned[:, HALF:], last], axis=1)


def narrow(x, nb):
    turned = pltpu.roll(x, FULL - (HALF - nb), 1)
    return jnp.where(iota((x.shape[0], 2 * nb), 1) < nb, x[:, : 2 * nb], turned[:, : 2 * nb])


def combine(prod):
    rows = prod.shape[0] // 2
    return (
        prod[:rows, :HALF] - prod[rows:, HALF:],
        prod[:rows, HALF:] + prod[rows:, :HALF],
    )


def halves(x):
    return jnp.concatenate([x[:, :HALF], x[:, HALF:]], axis=0)


def column(row):
    count = row.shape[1]
    same = iota((count, count), 0) == iota((count, count), 1)
    return jnp.sum(jnp.where(same, row, 0.0), axis=1, keepdims=True)


def kernel(
    n,
    owner_ref,
    slot_ref,
    off_ref,
    face_ref,
    adm_ref,
    weight_ref,
    src_ref,
    coupling_ref,
    inv_ref,
    liner_ref,
    state_ref,
    adjoint_ref,
    grad_ref,
    send,
    recv,
    adm_send,
    adm_recv,
    off_send,
    off_halo,
    grad_send,
    grad_recv,
    fields,
    w_fwd,
    w_adj,
    inv_pad,
    inv_herm,
    liner_pad,
    matrix,
    pick_fwd,
    pick_adj,
    src_sems,
    adm_sems,
    off_sems,
    grad_sems,
    halo_sems,
):
    me = lax.axis_index("mesh")
    elems = off_ref.shape[1]
    nb = inv_ref.shape[0]
    lin = adm_ref.shape[1]
    rows = src_ref.shape[0]

    def peer(k):
        return lax.rem(me + k, n)

    def to(src, dst, send_sem, recv_sem, p):
        return pltpu.make_async_remote_copy(
            src_ref=src,
            dst_ref=dst,
            send_sem=send_sem,
            recv_sem=recv_sem,
            device_id={"mesh": p},
            device_id_type=MESH,
        )

    def src_copy(p, owner):
        return to(send.at[p], recv.at[owner], src_sems.at[0, p], src_sems.at[1, owner], p)

    def adm_copy(p, owner):
        return to(adm_send, adm_recv.at[owner], adm_sems.at[0, p], adm_sems.at[1, owner], p)

    def grad_copy(p, owner):
        return to(
            grad_send.at[p], grad_recv.at[owner], grad_sems.at[0, p], grad_sems.at[1, owner], p
        )

    def off_copy(side, p):
        return to(off_send, off_halo.at[side], off_sems.at[0, side], off_sems.at[1, side], p)

    def halo_copy(step, side, p):
        own = pl.ds(elems - RIM if side == 0 else 0, RIM)
        there = pl.ds(elems if side == 0 else elems + RIM, RIM)
        return to(
            fields.at[step, own],
            fields.at[step, there],
            halo_sems.at[0, step, side],
            halo_sems.at[1, step, side],
            p,
        )

    up, down = jnp.minimum(me + 1, n - 1), jnp.maximum(me - 1, 0)
    has_up, has_down = me < n - 1, me > 0

    fields[...] = jnp.zeros_like(fields)
    off_halo[...] = jnp.zeros_like(off_halo)

    barrier = pltpu.get_barrier_semaphore()

    @pl.loop(1, n)
    def _(k):
        pl.semaphore_signal(barrier, inc=1, device_id={"mesh": peer(k)}, device_id_type=MESH)

    adm_send[...] = jnp.zeros_like(adm_send)
    adm_send[0:2, 0:lin] = adm_ref[...]
    off_send[...] = jnp.zeros_like(off_send)
    off_send[0:FACES, 0:elems] = off_ref[...].astype(F32)
    target = owner_ref[...] * elems + slot_ref[...]

    def partial_sum(p):
        pick = (iota((elems, rows), 0) + p * elems) == target
        return dot(pick.astype(F32).astype(BF16), src_ref[...])

    pl.semaphore_wait(barrier, n - 1)

    @pl.loop(1, n)
    def _(k):
        p = peer(k)
        send[p] = partial_sum(p).astype(BF16)
        src_copy(p, me).start()

    @pl.when(has_up)
    def _():
        off_copy(0, up).start()

    @pl.when(has_down)
    def _():
        off_copy(1, down).start()

    @pl.loop(1, n)
    def _(k):
        adm_copy(peer(k), me).start()

    def padded(x):
        wide = widen(x.astype(F32), nb)
        return jnp.concatenate([wide, jnp.zeros((HALF - nb, FULL), F32)], axis=0)

    inv_wide = padded(inv_ref[...])
    inv_pad[...] = inv_wide.astype(BF16)
    inv_herm[:, :HALF] = inv_wide[:, :HALF].T.astype(BF16)
    inv_herm[:, HALF:] = (-inv_wide[:, HALF:].T).astype(BF16)
    liner_pad[...] = padded(liner_ref[...]).astype(BF16)

    def fold(f):
        at = pl.ds(pl.multiple_of(f * HALF, HALF), HALF)
        re, im = combine(dot(halves(matrix[...]), inv_pad[...]))
        w_fwd[at, :HALF] = re.astype(BF16)
        w_fwd[at, HALF:] = im.astype(BF16)
        re, im = combine(dot(halves(inv_pad[...]), matrix[...]))
        w_adj[at, :HALF] = re.T.astype(BF16)
        w_adj[at, HALF:] = (-im.T).astype(BF16)

    @pl.loop(0, FACES)
    def _(f):
        matrix[...] = padded(coupling_ref[f]).astype(BF16)
        fold(f)

    matrix[...] = liner_pad[...]
    fold(FACES)

    lane = iota((128, 128), 1)
    place_row = jnp.where(
        lane < elems,
        lane,
        jnp.where(
            lane < elems + RIM,
            lane - elems - RIM,
            jnp.where(lane < elems + 2 * RIM, lane - RIM, -4096),
        ),
    ).astype(F32)
    place_col = place_row.T
    for f in range(FACES):
        meets = lane[:1].astype(F32) + off_send[f : f + 1, :]
        pick_fwd[f * elems : (f + 1) * elems, :] = (
            jnp.where(place_col == meets, 1.0, 0.0).T[:elems].astype(BF16)
        )

    @pl.when(has_down)
    def _():
        off_copy(0, down).wait_recv()

    @pl.when(has_up)
    def _():
        off_copy(1, up).wait_recv()

    lane8 = iota((8, 128), 1)
    offs = jnp.where(
        lane8 < elems,
        off_send[...],
        jnp.where(
            lane8 < elems + RIM,
            pltpu.roll(off_halo[0], RIM, 1),
            pltpu.roll(off_halo[1], elems + RIM, 1),
        ),
    )
    for f in range(FACES):
        lands = place_row[:1] + offs[f : f + 1, :]
        pick_adj[f * elems : (f + 1) * elems, :] = jnp.where(
            iota((elems, 128), 0).astype(F32) == lands, 1.0, 0.0
        ).astype(BF16)

    face = column(face_ref[...].astype(F32))
    weight = column(weight_ref[...])
    lane_e = iota((elems, 128), 1)

    def face_pick(p):
        return jnp.logical_and(face == (lane_e + p * lin).astype(F32), lane_e < lin)

    def admit(table, p, sums):
        pick = face_pick(p)
        return tuple(s + jnp.where(pick, table[i : i + 1, :], 0.0) for i, s in enumerate(sums))

    def admit_peer(k, sums):
        p = peer(n - k)
        adm_copy(p, p).wait_recv()
        return admit(adm_recv[p], p, sums)

    sums = admit(adm_send[...], me, (jnp.zeros((elems, 128), F32),) * 2)
    sums = lax.fori_loop(1, n, admit_peer, sums)
    y_re = jnp.sum(sums[0], axis=1, keepdims=True)
    y_im = jnp.sum(sums[1], axis=1, keepdims=True)

    def take(k, total):
        p = peer(n - k)
        src_copy(p, p).wait_recv()
        return total + recv[p].astype(F32)

    forcing = widen(lax.fori_loop(1, n, take, partial_sum(me)), nb)

    def sweeps(first, start, pick_ref, w_ref, yi):
        start_re, start_im = start
        now_re, now_im = start
        for s in range(first, first + SWEEPS):
            now = jnp.concatenate([now_re, now_im], axis=1).astype(BF16)
            fields[s, 0:elems, :] = now

            @pl.when(has_up)
            def _():
                halo_copy(s, 0, up).start()

            @pl.when(has_down)
            def _():
                halo_copy(s, 1, down).start()

            u = now.astype(F32)
            u_re, u_im = u[:, :HALF], u[:, HALF:]
            wall = jnp.concatenate(
                [y_re * u_re - yi * u_im, y_re * u_im + yi * u_re], axis=0
            ).astype(BF16)

            @pl.when(has_down)
            def _():
                halo_copy(s, 0, down).wait_recv()

            @pl.when(has_up)
            def _():
                halo_copy(s, 1, up).wait_recv()

            met = dot(pick_ref[...], fields[s]).astype(BF16)
            parts = [halves(met[f * elems : (f + 1) * elems]) for f in range(FACES)]
            left = jnp.concatenate(parts + [wall], axis=1)
            re, im = combine(dot(left, w_ref[...]))
            now_re, now_im = start_re - re, start_im - im
        return jnp.concatenate([now_re, now_im], axis=1).astype(BF16)

    start = combine(dot(halves(forcing.astype(BF16)), inv_pad[...]))
    state = sweeps(0, start, pick_fwd, w_fwd, y_im)
    state_f = state.astype(F32)
    state_ref[...] = narrow(state_f, nb).astype(BF16)
    source = weight * state_f
    start = combine(dot(halves(source.astype(BF16)), inv_herm[...]))
    adjoint = sweeps(SWEEPS, start, pick_adj, w_adj, -y_im)
    adjoint_f = adjoint.astype(F32)
    adjoint_ref[...] = narrow(adjoint_f, nb).astype(BF16)

    wall_re, wall_im = combine(dot(halves(state), liner_pad[...]))
    a, b = adjoint_f[:, :HALF], adjoint_f[:, HALF:]
    term_re = -jnp.sum(a * wall_re + b * wall_im, axis=1, keepdims=True) / 16.0
    term_im = -jnp.sum(b * wall_re - a * wall_im, axis=1, keepdims=True) / 16.0

    def grad_part(p):
        pick = face_pick(p)
        re = jnp.sum(jnp.where(pick, term_re, 0.0), axis=0, keepdims=True)
        im = jnp.sum(jnp.where(pick, term_im, 0.0), axis=0, keepdims=True)
        return jnp.concatenate([re, im, jnp.zeros((6, 128), F32)], axis=0)

    @pl.loop(1, n)
    def _(k):
        p = peer(k)
        grad_send[p] = grad_part(p)
        grad_copy(p, me).start()

    def take_grad(k, total):
        p = peer(n - k)
        grad_copy(p, p).wait_recv()
        return total + grad_recv[p]

    total = lax.fori_loop(1, n, take_grad, grad_part(me))
    grad_ref[...] = total[0:2, 0:lin]

    @pl.loop(1, n)
    def _(k):
        p = peer(k)
        src_copy(p, me).wait_send()
        adm_copy(p, me).wait_send()
        grad_copy(p, me).wait_send()

    @pl.when(has_up)
    def _():
        off_copy(0, up).wait_send()
        for s in range(2 * SWEEPS):
            halo_copy(s, 0, up).wait_send()

    @pl.when(has_down)
    def _():
        off_copy(1, down).wait_send()
        for s in range(2 * SWEEPS):
            halo_copy(s, 1, down).wait_send()


def solution(mesh):
    n = mesh.shape["mesh"]

    def local(
        src_rows,
        src_owner,
        src_slot,
        neighbour_offset,
        liner_face,
        admittance,
        observe_weight,
        coupling,
        block_inv,
        liner_op,
    ):
        rows, width = src_rows.shape
        elems = liner_face.shape[0]
        lin = admittance.shape[1]
        vmem = pl.BlockSpec(memory_space=pltpu.VMEM)
        dma = pltpu.SemaphoreType.DMA
        return tuple(
            pl.pallas_call(
                functools.partial(kernel, n),
                out_shape=(
                    jax.ShapeDtypeStruct((elems, width), BF16),
                    jax.ShapeDtypeStruct((elems, width), BF16),
                    jax.ShapeDtypeStruct((2, lin), F32),
                ),
                in_specs=[vmem] * 10,
                out_specs=(vmem,) * 3,
                scratch_shapes=[
                    pltpu.VMEM((n, elems, width), BF16),
                    pltpu.VMEM((n, elems, width), BF16),
                    pltpu.VMEM((8, 128), F32),
                    pltpu.VMEM((n, 8, 128), F32),
                    pltpu.VMEM((8, 128), F32),
                    pltpu.VMEM((2, 8, 128), F32),
                    pltpu.VMEM((n, 8, 128), F32),
                    pltpu.VMEM((n, 8, 128), F32),
                    pltpu.VMEM((2 * SWEEPS, 128, FULL), BF16),
                    pltpu.VMEM(((FACES + 1) * HALF, FULL), BF16),
                    pltpu.VMEM(((FACES + 1) * HALF, FULL), BF16),
                    pltpu.VMEM((HALF, FULL), BF16),
                    pltpu.VMEM((HALF, FULL), BF16),
                    pltpu.VMEM((HALF, FULL), BF16),
                    pltpu.VMEM((HALF, FULL), BF16),
                    pltpu.VMEM((FACES * elems, 128), BF16),
                    pltpu.VMEM((FACES * elems, 128), BF16),
                    dma((2, n)),
                    dma((2, n)),
                    dma((2, 2)),
                    dma((2, n)),
                    dma((2, 2 * SWEEPS, 2)),
                ],
                compiler_params=pltpu.CompilerParams(
                    collective_id=0, has_side_effects=True, vmem_limit_bytes=48 * 2**20
                ),
            )(
                src_owner.reshape(1, rows),
                src_slot.reshape(1, rows),
                neighbour_offset.T,
                liner_face.reshape(1, elems),
                admittance,
                observe_weight.reshape(1, elems),
                src_rows,
                coupling,
                block_inv,
                liner_op,
            )
        )

    placed = (
        P(("mode", "mesh"), None),
        P(("mode", "mesh"), None),
        P(("mode", "mesh")),
        P(("mode", "mesh"), None),
        P(("mode", "mesh")),
        P("mode", "mesh"),
        P(("mode", "mesh")),
        P("mode", None, None),
        P("mode", None),
        P("mode", None),
    )
    return jax.shard_map(
        local,
        mesh=mesh,
        in_specs=placed,
        out_specs=(P(("mode", "mesh"), None), P(("mode", "mesh"), None), P("mode", "mesh")),
        check_vma=False,
    )
```

```python
import functools

import jax
import jax.numpy as jnp
from jax import lax
from jax.experimental import pallas as pl
from jax.experimental.pallas import tpu as pltpu
from jax.sharding import PartitionSpec as P

SWEEPS = 4
RIM = 16
DEEP = 2 * RIM
FACES = 6
HALF = 384
FULL = 2 * HALF
MESH = pl.DeviceIdType.MESH
F32 = jnp.float32
BF16 = jnp.bfloat16


def iota(shape, dim):
    return lax.broadcasted_iota(jnp.int32, shape, dim)


def dot(a, b):
    return jnp.dot(a, b, preferred_element_type=F32)


def widen(x, nb):
    rows = x.shape[0]
    turned = pltpu.roll(x, HALF - nb, 1)
    wrap = 2 * (HALF - nb)
    real = jnp.where(iota((rows, HALF), 1) < nb, x[:, :HALF], 0.0)
    last = jnp.where(iota((rows, wrap), 1) < HALF - nb, turned[:, :wrap], 0.0)
    return jnp.concatenate([real, turned[:, HALF:], last], axis=1)


def narrow(x, nb):
    turned = pltpu.roll(x, FULL - (HALF - nb), 1)
    return jnp.where(iota((x.shape[0], 2 * nb), 1) < nb, x[:, : 2 * nb], turned[:, : 2 * nb])


def combine(prod):
    rows = prod.shape[0] // 2
    return (
        prod[:rows, :HALF] - prod[rows:, HALF:],
        prod[:rows, HALF:] + prod[rows:, :HALF],
    )


def halves(x):
    return jnp.concatenate([x[:, :HALF], x[:, HALF:]], axis=0)


def column(row):
    count = row.shape[1]
    same = iota((count, count), 0) == iota((count, count), 1)
    return jnp.sum(jnp.where(same, row, 0.0), axis=1, keepdims=True)


def kernel(
    n,
    owner_ref,
    slot_ref,
    off_ref,
    face_ref,
    adm_ref,
    weight_ref,
    src_ref,
    coupling_hbm,
    inv_hbm,
    liner_hbm,
    state_ref,
    adjoint_ref,
    grad_ref,
    send,
    recv,
    adm_send,
    adm_recv,
    off_send,
    off_halo,
    grad_send,
    grad_recv,
    fields,
    w_fwd,
    w_adj,
    inv_pad,
    inv_herm,
    liner_pad,
    matrix,
    pick_fwd,
    pick_adj,
    src_sems,
    adm_sems,
    off_sems,
    grad_sems,
    halo_sems,
    coupling_ref,
    inv_ref,
    liner_ref,
    load_sems,
):
    me = lax.axis_index("mesh")
    elems = off_ref.shape[1]
    nb = inv_ref.shape[0]
    lin = adm_ref.shape[1]
    rows = src_ref.shape[0]

    loads = [
        pltpu.make_async_copy(hbm, here, load_sems.at[i])
        for i, (hbm, here) in enumerate(
            ((inv_hbm, inv_ref), (liner_hbm, liner_ref), (coupling_hbm, coupling_ref))
        )
    ]
    for load in loads:
        load.start()

    def peer(k):
        return lax.rem(me + k, n)

    def to(src, dst, send_sem, recv_sem, p):
        return pltpu.make_async_remote_copy(
            src_ref=src,
            dst_ref=dst,
            send_sem=send_sem,
            recv_sem=recv_sem,
            device_id={"mesh": p},
            device_id_type=MESH,
        )

    def src_copy(p, owner):
        return to(send.at[p], recv.at[owner], src_sems.at[0, p], src_sems.at[1, owner], p)

    def adm_copy(p, owner):
        return to(adm_send, adm_recv.at[owner], adm_sems.at[0, p], adm_sems.at[1, owner], p)

    def grad_copy(p, owner):
        return to(
            grad_send.at[p], grad_recv.at[owner], grad_sems.at[0, p], grad_sems.at[1, owner], p
        )

    def off_copy(side, p):
        return to(off_send, off_halo.at[side], off_sems.at[0, side], off_sems.at[1, side], p)

    def halo_copy(step, side, p):
        own = pl.ds(elems - DEEP if side == 0 else 0, DEEP)
        there = pl.ds(elems if side == 0 else elems + DEEP, DEEP)
        return to(
            fields.at[step, own],
            fields.at[step, there],
            halo_sems.at[0, step // 2, side],
            halo_sems.at[1, step // 2, side],
            p,
        )

    up, down = jnp.minimum(me + 1, n - 1), jnp.maximum(me - 1, 0)
    has_up, has_down = me < n - 1, me > 0

    fields[...] = jnp.zeros_like(fields)
    off_halo[...] = jnp.zeros_like(off_halo)

    barrier = pltpu.get_barrier_semaphore()

    @pl.loop(1, n)
    def _(k):
        pl.semaphore_signal(barrier, inc=1, device_id={"mesh": peer(k)}, device_id_type=MESH)

    adm_send[...] = jnp.zeros_like(adm_send)
    adm_send[0:2, 0:lin] = adm_ref[...]
    off_send[...] = jnp.zeros_like(off_send)
    off_send[0:FACES, 0:elems] = off_ref[...].astype(F32)
    off_send[FACES : FACES + 1, 0:elems] = face_ref[...].astype(F32)
    target = owner_ref[...] * elems + slot_ref[...]

    def partial_sum(p):
        pick = (iota((elems, rows), 0) + p * elems) == target
        return dot(pick.astype(F32).astype(BF16), src_ref[...])

    pl.semaphore_wait(barrier, n - 1)

    @pl.loop(1, n)
    def _(k):
        p = peer(k)
        send[p] = partial_sum(p).astype(BF16)
        src_copy(p, me).start()

    @pl.when(has_up)
    def _():
        off_copy(0, up).start()

    @pl.when(has_down)
    def _():
        off_copy(1, down).start()

    @pl.loop(1, n)
    def _(k):
        adm_copy(peer(k), me).start()

    def padded(x):
        wide = widen(x.astype(F32), nb)
        return jnp.concatenate([wide, jnp.zeros((HALF - nb, FULL), F32)], axis=0)

    for load in loads:
        load.wait()
    inv_wide = padded(inv_ref[...])
    inv_pad[...] = inv_wide.astype(BF16)
    inv_herm[:, :HALF] = inv_wide[:, :HALF].T.astype(BF16)
    inv_herm[:, HALF:] = (-inv_wide[:, HALF:].T).astype(BF16)
    liner_pad[...] = padded(liner_ref[...]).astype(BF16)

    def fold(f):
        at = pl.ds(pl.multiple_of(f * HALF, HALF), HALF)
        re, im = combine(dot(halves(matrix[...]), inv_pad[...]))
        w_fwd[at, :HALF] = re.astype(BF16)
        w_fwd[at, HALF:] = im.astype(BF16)
        re, im = combine(dot(halves(inv_pad[...]), matrix[...]))
        w_adj[at, :HALF] = re.T.astype(BF16)
        w_adj[at, HALF:] = (-im.T).astype(BF16)

    @pl.loop(0, FACES)
    def _(f):
        matrix[...] = padded(coupling_ref[f]).astype(BF16)
        fold(f)

    matrix[...] = liner_pad[...]
    fold(FACES)

    @pl.when(has_down)
    def _():
        off_copy(0, down).wait_recv()

    @pl.when(has_up)
    def _():
        off_copy(1, up).wait_recv()

    lane8 = iota((8, 128), 1)
    offs = jnp.where(
        lane8 < elems,
        off_send[...],
        jnp.where(
            lane8 < elems + DEEP,
            pltpu.roll(off_halo[0], DEEP, 1),
            pltpu.roll(off_halo[1], elems + DEEP, 1),
        ),
    )
    lane = iota((128, 128), 1)
    place_row = jnp.where(
        lane < elems, lane, jnp.where(lane < elems + DEEP, lane - elems - DEEP, lane - DEEP)
    ).astype(F32)
    place_col = place_row.T
    near = elems + DEEP - RIM

    def kept(x):
        return jnp.concatenate([x[:elems], x[near : near + DEEP]], axis=0)

    for f in range(FACES):
        lands = jnp.where(place_col == place_row + offs[f : f + 1, :], 1.0, 0.0)
        pick_adj[f] = kept(lands).astype(BF16)
        pick_fwd[f] = kept(lands.T).astype(BF16)

    face_all = kept(column(offs[FACES : FACES + 1, :]))
    face = face_all[:elems]
    weight = column(weight_ref[...])
    lane_e = iota((elems, 128), 1)

    lane_a = iota((elems + DEEP, 128), 1)

    def face_pick(p):
        return jnp.logical_and(face == (lane_e + p * lin).astype(F32), lane_e < lin)

    def admit(table, p, sums):
        pick = jnp.logical_and(face_all == (lane_a + p * lin).astype(F32), lane_a < lin)
        return tuple(s + jnp.where(pick, table[i : i + 1, :], 0.0) for i, s in enumerate(sums))

    def admit_peer(k, sums):
        p = peer(n - k)
        adm_copy(p, p).wait_recv()
        return admit(adm_recv[p], p, sums)

    sums = admit(adm_send[...], me, (jnp.zeros((elems + DEEP, 128), F32),) * 2)
    sums = lax.fori_loop(1, n, admit_peer, sums)
    y_re = jnp.sum(sums[0], axis=1, keepdims=True)
    y_im = jnp.sum(sums[1], axis=1, keepdims=True)

    def take(k, total):
        p = peer(n - k)
        src_copy(p, p).wait_recv()
        return total + recv[p].astype(F32)

    forcing = widen(lax.fori_loop(1, n, take, partial_sum(me)), nb)

    def sweeps(first, start, pick_ref, w_ref, yi, beside):
        def sweep(s, pick, u, y_r, y_i):
            count = u.shape[0]
            u_re, u_im = u[:, :HALF], u[:, HALF:]
            wall = jnp.concatenate([y_r * u_re - y_i * u_im, y_r * u_im + y_i * u_re], axis=0)
            met = dot(pick.reshape(FACES * count, 128), fields[s]).astype(BF16)
            parts = [halves(met[f * count : (f + 1) * count]) for f in range(FACES)]
            left = jnp.concatenate(parts + [wall.astype(BF16)], axis=1)
            return jnp.concatenate(combine(dot(left, w_ref[...])), axis=1)

        start = jnp.concatenate(start, axis=1)
        now = start.astype(BF16)
        start_near = None
        for s in range(first, first + SWEEPS, 2):
            fields[s, 0:elems, :] = now

            @pl.when(has_up)
            def _():
                halo_copy(s, 0, up).start()

            @pl.when(has_down)
            def _():
                halo_copy(s, 1, down).start()

            if s == first:
                beside()

            @pl.when(has_down)
            def _():
                halo_copy(s, 0, down).wait_recv()

            @pl.when(has_up)
            def _():
                halo_copy(s, 1, up).wait_recv()

            halo = fields[s, near : near + DEEP, :].astype(F32)
            if start_near is None:
                start_near = jnp.concatenate([start, halo], axis=0)
            u = jnp.concatenate([now.astype(F32), halo], axis=0)
            now = (start_near - sweep(s, pick_ref[...], u, y_re, yi)).astype(BF16)
            fields[s + 1, 0:elems, :] = now[:elems]
            fields[s + 1, near : near + DEEP, :] = now[elems:]
            u = now[:elems].astype(F32)
            now = start - sweep(s + 1, pick_ref[:, 0:elems, :], u, y_re[:elems], yi[:elems])
            now = now.astype(BF16)
        return now

    start = combine(dot(halves(forcing.astype(BF16)), inv_pad[...]))
    state = sweeps(0, start, pick_fwd, w_fwd, y_im, lambda: None)
    state_f = state.astype(F32)
    source = weight * state_f
    start = combine(dot(halves(source.astype(BF16)), inv_herm[...]))
    walls = []

    def beside():
        state_ref[...] = narrow(state_f, nb).astype(BF16)
        walls.extend(combine(dot(halves(state), liner_pad[...])))

    adjoint = sweeps(SWEEPS, start, pick_adj, w_adj, -y_im, beside)
    adjoint_f = adjoint.astype(F32)
    wall_re, wall_im = walls
    a, b = adjoint_f[:, :HALF], adjoint_f[:, HALF:]
    term_re = -jnp.sum(a * wall_re + b * wall_im, axis=1, keepdims=True) / 16.0
    term_im = -jnp.sum(b * wall_re - a * wall_im, axis=1, keepdims=True) / 16.0

    def grad_part(p):
        pick = face_pick(p)
        re = jnp.sum(jnp.where(pick, term_re, 0.0), axis=0, keepdims=True)
        im = jnp.sum(jnp.where(pick, term_im, 0.0), axis=0, keepdims=True)
        return jnp.concatenate([re, im, jnp.zeros((6, 128), F32)], axis=0)

    @pl.loop(1, n)
    def _(k):
        p = peer(k)
        grad_send[p] = grad_part(p)
        grad_copy(p, me).start()

    def take_grad(k, total):
        p = peer(n - k)
        grad_copy(p, p).wait_recv()
        return total + grad_recv[p]

    adjoint_ref[...] = narrow(adjoint_f, nb).astype(BF16)
    total = lax.fori_loop(1, n, take_grad, grad_part(me))
    grad_ref[...] = total[0:2, 0:lin]

    @pl.loop(1, n)
    def _(k):
        p = peer(k)
        src_copy(p, me).wait_send()
        adm_copy(p, me).wait_send()
        grad_copy(p, me).wait_send()

    @pl.when(has_up)
    def _():
        off_copy(0, up).wait_send()
        for s in range(0, 2 * SWEEPS, 2):
            halo_copy(s, 0, up).wait_send()

    @pl.when(has_down)
    def _():
        off_copy(1, down).wait_send()
        for s in range(0, 2 * SWEEPS, 2):
            halo_copy(s, 1, down).wait_send()


def solution(mesh):
    n = mesh.shape["mesh"]

    def local(
        src_rows,
        src_owner,
        src_slot,
        neighbour_offset,
        liner_face,
        admittance,
        observe_weight,
        coupling,
        block_inv,
        liner_op,
    ):
        rows, width = src_rows.shape
        elems = liner_face.shape[0]
        lin = admittance.shape[1]
        vmem = pl.BlockSpec(memory_space=pltpu.VMEM)
        dma = pltpu.SemaphoreType.DMA
        return tuple(
            pl.pallas_call(
                functools.partial(kernel, n),
                out_shape=(
                    jax.ShapeDtypeStruct((elems, width), BF16),
                    jax.ShapeDtypeStruct((elems, width), BF16),
                    jax.ShapeDtypeStruct((2, lin), F32),
                ),
                in_specs=[vmem] * 7 + [pl.BlockSpec(memory_space=pltpu.HBM)] * 3,
                out_specs=(vmem,) * 3,
                scratch_shapes=[
                    pltpu.VMEM((n, elems, width), BF16),
                    pltpu.VMEM((n, elems, width), BF16),
                    pltpu.VMEM((8, 128), F32),
                    pltpu.VMEM((n, 8, 128), F32),
                    pltpu.VMEM((8, 128), F32),
                    pltpu.VMEM((2, 8, 128), F32),
                    pltpu.VMEM((n, 8, 128), F32),
                    pltpu.VMEM((n, 8, 128), F32),
                    pltpu.VMEM((2 * SWEEPS, 128, FULL), BF16),
                    pltpu.VMEM(((FACES + 1) * HALF, FULL), BF16),
                    pltpu.VMEM(((FACES + 1) * HALF, FULL), BF16),
                    pltpu.VMEM((HALF, FULL), BF16),
                    pltpu.VMEM((HALF, FULL), BF16),
                    pltpu.VMEM((HALF, FULL), BF16),
                    pltpu.VMEM((HALF, FULL), BF16),
                    pltpu.VMEM((FACES, elems + DEEP, 128), BF16),
                    pltpu.VMEM((FACES, elems + DEEP, 128), BF16),
                    dma((2, n)),
                    dma((2, n)),
                    dma((2, 2)),
                    dma((2, n)),
                    dma((2, SWEEPS, 2)),
                    pltpu.VMEM(coupling.shape, BF16),
                    pltpu.VMEM(block_inv.shape, BF16),
                    pltpu.VMEM(liner_op.shape, BF16),
                    dma((3,)),
                ],
                compiler_params=pltpu.CompilerParams(
                    collective_id=0, has_side_effects=True, vmem_limit_bytes=2**26 - 2**16
                ),
            )(
                src_owner.reshape(1, rows),
                src_slot.reshape(1, rows),
                neighbour_offset.T,
                liner_face.reshape(1, elems),
                admittance,
                observe_weight.reshape(1, elems),
                src_rows,
                coupling,
                block_inv,
                liner_op,
            )
        )

    placed = (
        P(("mode", "mesh"), None),
        P(("mode", "mesh"), None),
        P(("mode", "mesh")),
        P(("mode", "mesh"), None),
        P(("mode", "mesh")),
        P("mode", "mesh"),
        P(("mode", "mesh")),
        P("mode", None, None),
        P("mode", None),
        P("mode", None),
    )
    return jax.shard_map(
        local,
        mesh=mesh,
        in_specs=placed,
        out_specs=(P(("mode", "mesh"), None), P(("mode", "mesh"), None), P("mode", "mesh")),
        check_vma=False,
    )
```

```python
import functools

import jax
import jax.numpy as jnp
from jax import lax
from jax.experimental import pallas as pl
from jax.experimental.pallas import tpu as pltpu
from jax.sharding import PartitionSpec as P

SWEEPS = 4
RIM = 16
DEEP = 2 * RIM
FACES = 6
HALF = 384
FULL = 2 * HALF
MESH = pl.DeviceIdType.MESH
F32 = jnp.float32
BF16 = jnp.bfloat16


def iota(shape, dim):
    return lax.broadcasted_iota(jnp.int32, shape, dim)


def dot(a, b):
    return jnp.dot(a, b, preferred_element_type=F32)


def widen(x, nb):
    rows = x.shape[0]
    turned = pltpu.roll(x, HALF - nb, 1)
    wrap = 2 * (HALF - nb)
    real = jnp.where(iota((rows, HALF), 1) < nb, x[:, :HALF], 0.0)
    last = jnp.where(iota((rows, wrap), 1) < HALF - nb, turned[:, :wrap], 0.0)
    return jnp.concatenate([real, turned[:, HALF:], last], axis=1)


def narrow(x, nb):
    turned = pltpu.roll(x, FULL - (HALF - nb), 1)
    return jnp.where(iota((x.shape[0], 2 * nb), 1) < nb, x[:, : 2 * nb], turned[:, : 2 * nb])


def combine(prod):
    rows = prod.shape[0] // 2
    return (
        prod[:rows, :HALF] - prod[rows:, HALF:],
        prod[:rows, HALF:] + prod[rows:, :HALF],
    )


def halves(x):
    return jnp.concatenate([x[:, :HALF], x[:, HALF:]], axis=0)


def column(row):
    count = row.shape[1]
    same = iota((count, count), 0) == iota((count, count), 1)
    return jnp.sum(jnp.where(same, row, 0.0), axis=1, keepdims=True)


def kernel(
    n,
    owner_ref,
    slot_ref,
    off_ref,
    face_ref,
    adm_ref,
    weight_ref,
    src_ref,
    coupling_hbm,
    inv_hbm,
    liner_hbm,
    state_ref,
    adjoint_ref,
    grad_ref,
    send,
    recv,
    adm_send,
    adm_recv,
    off_send,
    off_halo,
    grad_send,
    grad_recv,
    fields,
    w_fwd,
    w_adj,
    inv_pad,
    inv_herm,
    liner_pad,
    matrix,
    pick_fwd,
    pick_adj,
    src_sems,
    adm_sems,
    off_sems,
    grad_sems,
    halo_sems,
    coupling_ref,
    inv_ref,
    liner_ref,
    load_sems,
):
    me = lax.axis_index("mesh")
    elems = off_ref.shape[1]
    nb = inv_ref.shape[0]
    lin = adm_ref.shape[1]
    rows = src_ref.shape[0]

    loads = [
        pltpu.make_async_copy(hbm, here, load_sems.at[i])
        for i, (hbm, here) in enumerate(
            ((inv_hbm, inv_ref), (liner_hbm, liner_ref), (coupling_hbm, coupling_ref))
        )
    ]
    for load in loads:
        load.start()

    def peer(k):
        return lax.rem(me + k, n)

    def to(src, dst, send_sem, recv_sem, p):
        return pltpu.make_async_remote_copy(
            src_ref=src,
            dst_ref=dst,
            send_sem=send_sem,
            recv_sem=recv_sem,
            device_id={"mesh": p},
            device_id_type=MESH,
        )

    def src_copy(p, owner):
        return to(send.at[p], recv.at[owner], src_sems.at[0, p], src_sems.at[1, owner], p)

    def adm_copy(p, owner):
        return to(adm_send, adm_recv.at[owner], adm_sems.at[0, p], adm_sems.at[1, owner], p)

    def grad_copy(p, owner):
        return to(
            grad_send.at[p], grad_recv.at[owner], grad_sems.at[0, p], grad_sems.at[1, owner], p
        )

    def off_copy(side, p):
        return to(off_send, off_halo.at[side], off_sems.at[0, side], off_sems.at[1, side], p)

    def halo_copy(step, side, p):
        own = pl.ds(elems - DEEP if side == 0 else 0, DEEP)
        there = pl.ds(elems if side == 0 else elems + DEEP, DEEP)
        return to(
            fields.at[step, own],
            fields.at[step, there],
            halo_sems.at[0, step // 2, side],
            halo_sems.at[1, step // 2, side],
            p,
        )

    up, down = jnp.minimum(me + 1, n - 1), jnp.maximum(me - 1, 0)
    has_up, has_down = me < n - 1, me > 0

    fields[...] = jnp.zeros_like(fields)
    off_halo[...] = jnp.zeros_like(off_halo)

    barrier = pltpu.get_barrier_semaphore()

    @pl.loop(1, n)
    def _(k):
        pl.semaphore_signal(barrier, inc=1, device_id={"mesh": peer(k)}, device_id_type=MESH)

    adm_send[...] = jnp.zeros_like(adm_send)
    adm_send[0:2, 0:lin] = adm_ref[...]
    off_send[...] = jnp.zeros_like(off_send)
    off_send[0:FACES, 0:elems] = off_ref[...].astype(F32)
    off_send[FACES : FACES + 1, 0:elems] = face_ref[...].astype(F32)
    target = owner_ref[...] * elems + slot_ref[...]

    def partial_sum(p):
        pick = (iota((elems, rows), 0) + p * elems) == target
        return dot(pick.astype(F32).astype(BF16), src_ref[...])

    @pl.loop(1, n)
    def _(k):
        p = peer(k)
        send[p] = partial_sum(p).astype(BF16)

    pl.semaphore_wait(barrier, n - 1)

    @pl.loop(1, n)
    def _(k):
        src_copy(peer(k), me).start()

    @pl.when(has_up)
    def _():
        off_copy(0, up).start()

    @pl.when(has_down)
    def _():
        off_copy(1, down).start()

    @pl.loop(1, n)
    def _(k):
        adm_copy(peer(k), me).start()

    def padded(x):
        wide = widen(x.astype(F32), nb)
        return jnp.concatenate([wide, jnp.zeros((HALF - nb, FULL), F32)], axis=0)

    for load in loads:
        load.wait()
    inv_wide = padded(inv_ref[...])
    inv_pad[...] = inv_wide.astype(BF16)
    inv_herm[:, :HALF] = inv_wide[:, :HALF].T.astype(BF16)
    inv_herm[:, HALF:] = (-inv_wide[:, HALF:].T).astype(BF16)
    liner_pad[...] = padded(liner_ref[...]).astype(BF16)

    def fold(f):
        at = pl.ds(pl.multiple_of(f * HALF, HALF), HALF)
        re, im = combine(dot(halves(matrix[...]), inv_pad[...]))
        w_fwd[at, :HALF] = re.astype(BF16)
        w_fwd[at, HALF:] = im.astype(BF16)
        re, im = combine(dot(halves(inv_pad[...]), matrix[...]))
        w_adj[at, :HALF] = re.T.astype(BF16)
        w_adj[at, HALF:] = (-im.T).astype(BF16)

    @pl.loop(0, FACES)
    def _(f):
        matrix[...] = padded(coupling_ref[f]).astype(BF16)
        fold(f)

    matrix[...] = liner_pad[...]
    fold(FACES)

    @pl.when(has_down)
    def _():
        off_copy(0, down).wait_recv()

    @pl.when(has_up)
    def _():
        off_copy(1, up).wait_recv()

    lane8 = iota((8, 128), 1)
    offs = jnp.where(
        lane8 < elems,
        off_send[...],
        jnp.where(
            lane8 < elems + DEEP,
            pltpu.roll(off_halo[0], DEEP, 1),
            pltpu.roll(off_halo[1], elems + DEEP, 1),
        ),
    )
    lane = iota((128, 128), 1)
    place_row = jnp.where(
        lane < elems, lane, jnp.where(lane < elems + DEEP, lane - elems - DEEP, lane - DEEP)
    ).astype(F32)
    place_col = place_row.T
    near = elems + DEEP - RIM

    def kept(x):
        return jnp.concatenate([x[:elems], x[near : near + DEEP]], axis=0)

    for f in range(FACES):
        lands = jnp.where(place_col == place_row + offs[f : f + 1, :], 1.0, 0.0)
        pick_adj[f] = kept(lands).astype(BF16)
        pick_fwd[f] = kept(lands.T).astype(BF16)

    face_all = kept(column(offs[FACES : FACES + 1, :]))
    face = face_all[:elems]
    weight = column(weight_ref[...])
    lane_e = iota((elems, 128), 1)

    lane_a = iota((elems + DEEP, 128), 1)

    def face_pick(p):
        return jnp.logical_and(face == (lane_e + p * lin).astype(F32), lane_e < lin)

    def admit(table, p, sums):
        pick = jnp.logical_and(face_all == (lane_a + p * lin).astype(F32), lane_a < lin)
        return tuple(s + jnp.where(pick, table[i : i + 1, :], 0.0) for i, s in enumerate(sums))

    def admit_peer(k, sums):
        p = peer(n - k)
        adm_copy(p, p).wait_recv()
        return admit(adm_recv[p], p, sums)

    sums = admit(adm_send[...], me, (jnp.zeros((elems + DEEP, 128), F32),) * 2)
    sums = lax.fori_loop(1, n, admit_peer, sums)
    y_re = jnp.sum(sums[0], axis=1, keepdims=True)
    y_im = jnp.sum(sums[1], axis=1, keepdims=True)

    def take(k, total):
        p = peer(n - k)
        src_copy(p, p).wait_recv()
        return total + recv[p].astype(F32)

    forcing = widen(lax.fori_loop(1, n, take, partial_sum(me)), nb)

    def sweeps(first, start, pick_ref, w_ref, yi, beside):
        def sweep(s, pick, u, y_r, y_i):
            count = u.shape[0]
            u_re, u_im = u[:, :HALF], u[:, HALF:]
            wall = jnp.concatenate([y_r * u_re - y_i * u_im, y_r * u_im + y_i * u_re], axis=0)
            met = dot(pick.reshape(FACES * count, 128), fields[s]).astype(BF16)
            parts = [halves(met[f * count : (f + 1) * count]) for f in range(FACES)]
            left = jnp.concatenate(parts + [wall.astype(BF16)], axis=1)
            return jnp.concatenate(combine(dot(left, w_ref[...])), axis=1)

        start = jnp.concatenate(start, axis=1)
        now = start.astype(BF16)
        start_near = None
        for s in range(first, first + SWEEPS, 2):
            fields[s, 0:elems, :] = now

            @pl.when(has_up)
            def _():
                halo_copy(s, 0, up).start()

            @pl.when(has_down)
            def _():
                halo_copy(s, 1, down).start()

            if s == first:
                beside()

            @pl.when(has_down)
            def _():
                halo_copy(s, 0, down).wait_recv()

            @pl.when(has_up)
            def _():
                halo_copy(s, 1, up).wait_recv()

            halo = fields[s, near : near + DEEP, :].astype(F32)
            if start_near is None:
                start_near = jnp.concatenate([start, halo], axis=0)
            u = jnp.concatenate([now.astype(F32), halo], axis=0)
            now = (start_near - sweep(s, pick_ref[...], u, y_re, yi)).astype(BF16)
            fields[s + 1, 0:elems, :] = now[:elems]
            fields[s + 1, near : near + DEEP, :] = now[elems:]
            u = now[:elems].astype(F32)
            now = start - sweep(s + 1, pick_ref[:, 0:elems, :], u, y_re[:elems], yi[:elems])
            now = now.astype(BF16)
        return now

    start = combine(dot(halves(forcing.astype(BF16)), inv_pad[...]))
    state = sweeps(0, start, pick_fwd, w_fwd, y_im, lambda: None)
    state_f = state.astype(F32)
    source = weight * state_f
    start = combine(dot(halves(source.astype(BF16)), inv_herm[...]))
    walls = []

    def beside():
        state_ref[...] = narrow(state_f, nb).astype(BF16)
        walls.extend(combine(dot(halves(state), liner_pad[...])))

    adjoint = sweeps(SWEEPS, start, pick_adj, w_adj, -y_im, beside)
    adjoint_f = adjoint.astype(F32)
    wall_re, wall_im = walls
    a, b = adjoint_f[:, :HALF], adjoint_f[:, HALF:]
    term_re = -jnp.sum(a * wall_re + b * wall_im, axis=1, keepdims=True) / 16.0
    term_im = -jnp.sum(b * wall_re - a * wall_im, axis=1, keepdims=True) / 16.0

    def grad_part(p):
        pick = face_pick(p)
        re = jnp.sum(jnp.where(pick, term_re, 0.0), axis=0, keepdims=True)
        im = jnp.sum(jnp.where(pick, term_im, 0.0), axis=0, keepdims=True)
        return jnp.concatenate([re, im, jnp.zeros((6, 128), F32)], axis=0)

    @pl.loop(1, n)
    def _(k):
        p = peer(k)
        grad_send[p] = grad_part(p)
        grad_copy(p, me).start()

    def take_grad(k, total):
        p = peer(n - k)
        grad_copy(p, p).wait_recv()
        return total + grad_recv[p]

    adjoint_ref[...] = narrow(adjoint_f, nb).astype(BF16)
    total = lax.fori_loop(1, n, take_grad, grad_part(me))
    grad_ref[...] = total[0:2, 0:lin]

    @pl.loop(1, n)
    def _(k):
        p = peer(k)
        src_copy(p, me).wait_send()
        adm_copy(p, me).wait_send()
        grad_copy(p, me).wait_send()

    @pl.when(has_up)
    def _():
        off_copy(0, up).wait_send()
        for s in range(0, 2 * SWEEPS, 2):
            halo_copy(s, 0, up).wait_send()

    @pl.when(has_down)
    def _():
        off_copy(1, down).wait_send()
        for s in range(0, 2 * SWEEPS, 2):
            halo_copy(s, 1, down).wait_send()


def solution(mesh):
    n = mesh.shape["mesh"]

    def local(
        src_rows,
        src_owner,
        src_slot,
        neighbour_offset,
        liner_face,
        admittance,
        observe_weight,
        coupling,
        block_inv,
        liner_op,
    ):
        rows, width = src_rows.shape
        elems = liner_face.shape[0]
        lin = admittance.shape[1]
        vmem = pl.BlockSpec(memory_space=pltpu.VMEM)
        dma = pltpu.SemaphoreType.DMA
        return tuple(
            pl.pallas_call(
                functools.partial(kernel, n),
                out_shape=(
                    jax.ShapeDtypeStruct((elems, width), BF16),
                    jax.ShapeDtypeStruct((elems, width), BF16),
                    jax.ShapeDtypeStruct((2, lin), F32),
                ),
                in_specs=[vmem] * 7 + [pl.BlockSpec(memory_space=pltpu.HBM)] * 3,
                out_specs=(vmem,) * 3,
                scratch_shapes=[
                    pltpu.VMEM((n, elems, width), BF16),
                    pltpu.VMEM((n, elems, width), BF16),
                    pltpu.VMEM((8, 128), F32),
                    pltpu.VMEM((n, 8, 128), F32),
                    pltpu.VMEM((8, 128), F32),
                    pltpu.VMEM((2, 8, 128), F32),
                    pltpu.VMEM((n, 8, 128), F32),
                    pltpu.VMEM((n, 8, 128), F32),
                    pltpu.VMEM((2 * SWEEPS, 128, FULL), BF16),
                    pltpu.VMEM(((FACES + 1) * HALF, FULL), BF16),
                    pltpu.VMEM(((FACES + 1) * HALF, FULL), BF16),
                    pltpu.VMEM((HALF, FULL), BF16),
                    pltpu.VMEM((HALF, FULL), BF16),
                    pltpu.VMEM((HALF, FULL), BF16),
                    pltpu.VMEM((HALF, FULL), BF16),
                    pltpu.VMEM((FACES, elems + DEEP, 128), BF16),
                    pltpu.VMEM((FACES, elems + DEEP, 128), BF16),
                    dma((2, n)),
                    dma((2, n)),
                    dma((2, 2)),
                    dma((2, n)),
                    dma((2, SWEEPS, 2)),
                    pltpu.VMEM(coupling.shape, BF16),
                    pltpu.VMEM(block_inv.shape, BF16),
                    pltpu.VMEM(liner_op.shape, BF16),
                    dma((3,)),
                ],
                compiler_params=pltpu.CompilerParams(
                    collective_id=0, has_side_effects=True, vmem_limit_bytes=2**26 - 2**16
                ),
            )(
                src_owner.reshape(1, rows),
                src_slot.reshape(1, rows),
                neighbour_offset.T,
                liner_face.reshape(1, elems),
                admittance,
                observe_weight.reshape(1, elems),
                src_rows,
                coupling,
                block_inv,
                liner_op,
            )
        )

    placed = (
        P(("mode", "mesh"), None),
        P(("mode", "mesh"), None),
        P(("mode", "mesh")),
        P(("mode", "mesh"), None),
        P(("mode", "mesh")),
        P("mode", "mesh"),
        P(("mode", "mesh")),
        P("mode", None, None),
        P("mode", None),
        P("mode", None),
    )
    return jax.shard_map(
        local,
        mesh=mesh,
        in_specs=placed,
        out_specs=(P(("mode", "mesh"), None), P(("mode", "mesh"), None), P("mode", "mesh")),
        check_vma=False,
    )
```
